128 devices in a mesh: gr: 8 (over z, y_lo), gc: 16 (over x, y_hi, core).
Axes of the slice: x: 4, y: 4 (y_hi: 2, y_lo: 2; y = y_hi * 2 + y_lo), z: 4, core: 2. Of those that a mesh axis runs over, the one named last changes fastest.
Arguments:
- embeddings: bfloat16 [32768, 768], P(('gr', 'gc'))
- cluster_ids: int32 [32768], P(('gr', 'gc')), may hold values from 0 to 7, as said below
Outputs:
- neighbour_sum: float32 [32768, 768], P(('gr', 'gc'))
- density: float32 [32768], P(('gr', 'gc'))
The draws below stay inside these ranges and needn't reach their ends.
Inputs may be any that keep to these rules, and one draw needn't show every extreme that they name: `cluster_ids`: each device's 256 rows hold exactly 32 rows of every cluster.
All inputs are finite; a program needn't handle non-finite values.
Results may differ from the reference program's by a relative error of at most 0.0017.
Values may be sent and summed in bfloat16 or wider, within the bound.
A program may use at most 128 MiB of HBM per device.

```python
import math
import jax
import jax.numpy as jnp
from jax import lax

D = 768
R_DEV = 256
CLUSTERS = 8
ROWS = 32768


def shared_ids(key):
    blocks = ROWS // R_DEV
    base = jnp.tile(jnp.arange(CLUSTERS, dtype=jnp.int32), R_DEV // CLUSTERS)
    keys = jax.random.split(jax.random.fold_in(key, 11), blocks)
    mixed = jax.vmap(lambda k: jax.random.permutation(k, base))(keys)
    return mixed.reshape(ROWS).astype(jnp.int32)


def draw_cluster_ids(key, part):
    return shared_ids(key)


def draw_embeddings(key, part):
    ids = shared_ids(key)
    centres = jax.random.normal(jax.random.fold_in(key, 7), (CLUSTERS, D), jnp.float32)
    noise = jax.random.normal(jax.random.fold_in(key, 13), (ROWS, D), jnp.float32)
    values = 0.8 * centres[ids] + 0.6 * noise
    return values.astype(jnp.bfloat16)


def setup_inputs(seed: int = 0) -> dict:
    key_of = jax.random.split(jax.random.key(seed), 3)
    embeddings = draw_embeddings(jax.random.fold_in(key_of[2], 71), 0)
    cluster_ids = draw_cluster_ids(jax.random.fold_in(key_of[2], 71), 0)
    return {"embeddings": embeddings, "cluster_ids": cluster_ids}


beta_scale = 16.0

def inverse_norms(embeddings):
    wide = embeddings.astype(jnp.float32)
    return lax.rsqrt(lax.optimization_barrier(jnp.sum(wide * wide, axis=1)) + 1e-06)

def reference(embeddings, cluster_ids):
    inv = inverse_norms(embeddings)
    block = math.gcd(ROWS, 2048)
    row_blocks = embeddings.reshape(ROWS // block, block, D)
    inv_blocks = inv.reshape(ROWS // block, block)
    id_blocks = cluster_ids.reshape(ROWS // block, block)

    def one_block(triple):
        rows, row_inv, row_ids = triple
        raw = jnp.dot(rows, embeddings.T, preferred_element_type=jnp.float32)
        sim = raw * row_inv[:, None] * inv[None, :]
        weight = jnp.where(row_ids[:, None] == cluster_ids[None, :], jnp.exp(beta_scale * (sim - 1.0)), jnp.float32(0.0))
        dens = lax.optimization_barrier(jnp.sum(weight, axis=1))
        coef = (weight * inv[None, :]).astype(jnp.bfloat16)
        total = jnp.dot(coef, embeddings, preferred_element_type=jnp.float32)
        return (total, dens)
    totals, denses = lax.map(one_block, (row_blocks, inv_blocks, id_blocks))
    return (totals.reshape(ROWS, D), denses.reshape(ROWS))
```

```python
import functools

import jax
import jax.numpy as jnp
from jax import lax
from jax.experimental import pallas as pl
from jax.experimental.pallas import tpu as pltpu
from jax.sharding import PartitionSpec as P

MESH = pl.DeviceIdType.MESH
F32 = jnp.float32
BF16 = jnp.bfloat16

beta_scale = 16.0
ROWS = 256
D = 768
PARTS = 3
W = D // PARTS
SLICE = 32
HALF = ROWS // 2
ORDER = (0, 1, 2, 4, 3, 5, 6, 7)


def place():
    gr, gc = lax.axis_index("gr"), lax.axis_index("gc")
    x = gc // 4
    y = ((gc // 2) % 2) * 2 + gr % 2
    z = gr // 2
    return x, y, z, gc % 2


def device(x, y, z, core):
    return (z * 2 + y % 2, x * 4 + (y // 2) * 2 + core)


def near(v):
    return v + 1 - 2 * (v % 2)


def far(v):
    return 3 - v


def link_items():
    items = [[(b, 0), ((b + 2) % 3, 0), ((b + 1) % 3, 0)] for b in range(3)]
    for b in range(3):
        p1, p2 = (b + 2) % 3, (b + 1) % 3
        b1, b2 = 1 << p1, 1 << p2
        items[b] += [(p1, b1), (p2, b2), (p2, b1), (p2, b1 | b2)]
    return items


def to_lanes(column):
    return jnp.transpose(jnp.broadcast_to(column, (column.shape[0], 128)))[0:1, :]


def to_column(row):
    return jnp.transpose(jnp.broadcast_to(row, (128, row.shape[1])))[:, 0:1]


def kernel(
    e_ref, ids_ref, out_ref, dens_ref,
    sorted_ref, held, acc, dacc, perm, perm_t, inv_ref, coded, pay, back, back_pay,
    deliver_send, deliver_recv, link_send, link_recv, core_send, core_recv,
    ret_send, ret_recv, pay_send, pay_recv,
):
    x, y, z, core = place()
    here = (x, y, z)
    outer = []
    for s in range(8):
        t = [far(here[a]) if (ORDER[s] >> a) & 1 else here[a] for a in range(3)]
        outer.append(device(*t, core))
    inner = []
    for a in range(3):
        t = [near(here[i]) if i == a else here[i] for i in range(3)]
        inner.append(device(*t, core))
    sibling = device(x, y, z, 1 - core)

    barrier = pltpu.get_barrier_semaphore()
    for d in outer[1:] + inner + [sibling]:
        pl.semaphore_signal(barrier, inc=1, device_id=d, device_id_type=MESH)

    mine = x // 2 + 2 * (y // 2) + 4 * (z // 2)
    rel = jnp.bitwise_xor(ids_ref[...], mine)
    slot = jnp.where(rel == 3, 4, jnp.where(rel == 4, 3, rel)).astype(F32)
    slot_col = to_column(slot)
    i0 = lax.broadcasted_iota(jnp.int32, (ROWS, ROWS), 0)
    i1 = lax.broadcasted_iota(jnp.int32, (ROWS, ROWS), 1)
    earlier = jnp.where((slot_col == slot) & (i0 < i1), F32(1.0), F32(0.0))
    pos = slot * SLICE + jnp.sum(earlier, axis=0, keepdims=True)
    p = jnp.where(i0.astype(F32) == pos, F32(1.0), F32(0.0)).astype(BF16)
    perm[...] = p
    for part in range(PARTS):
        rows = jnp.dot(p, e_ref[:, part * W:(part + 1) * W], preferred_element_type=F32).astype(BF16)
        sorted_ref[part] = rows
        held[0, part, 0, 0:SLICE, :] = rows[0:SLICE]

    pl.semaphore_wait(barrier, 11)

    def deliver(s):
        return pltpu.make_async_remote_copy(
            src_ref=sorted_ref.at[:, pl.ds(s * SLICE, SLICE), :],
            dst_ref=held.at[0, :, 0, pl.ds(s * SLICE, SLICE), :],
            send_sem=deliver_send.at[s], recv_sem=deliver_recv.at[s],
            device_id=outer[s], device_id_type=MESH)

    items = link_items()

    def over_link(b, k, half):
        part, h = items[b][k]
        rows = pl.ds(half * HALF, HALF)
        return pltpu.make_async_remote_copy(
            src_ref=held.at[0, part, h, rows, :],
            dst_ref=held.at[0, part, h ^ (1 << b), rows, :],
            send_sem=link_send.at[b, k, half], recv_sem=link_recv.at[b, k, half],
            device_id=inner[b], device_id_type=MESH)

    def to_sibling(h):
        return pltpu.make_async_remote_copy(
            src_ref=held.at[0, :, h], dst_ref=held.at[1, :, h],
            send_sem=core_send.at[h], recv_sem=core_recv.at[h],
            device_id=sibling, device_id_type=MESH)

    def arrive(b, k, half):
        over_link(b, k, half).wait_recv()
        part, h = items[b][k]
        h ^= 1 << b
        for d in range(3):
            if (part, h) in items[d]:
                over_link(d, items[d].index((part, h)), half).start()

    def absorb(c, h, first=False):
        cols = [held[c, part, h] for part in range(PARTS)]
        raw = None
        squares = None
        for part in range(PARTS):
            r = lax.dot_general(held[0, part, 0], cols[part], (((1,), (1,)), ((), ())),
                                preferred_element_type=F32)
            wide = cols[part].astype(F32)
            q = jnp.sum(wide * wide, axis=1, keepdims=True)
            raw = r if raw is None else raw + r
            squares = q if squares is None else squares + q
        inv = lax.rsqrt(squares + 1e-06)
        if first:
            inv_ref[...] = jnp.broadcast_to(inv, (ROWS, 128))
        inv_lanes = to_lanes(inv)
        sim = raw * inv_ref[:, 0:1] * inv_lanes
        weight = jnp.exp(beta_scale * (sim - 1.0))
        dens = weight[:, :128] + weight[:, 128:]
        coef = (weight * inv_lanes).astype(BF16)
        dacc[...] = dens if first else dacc[...] + dens
        for part in range(PARTS):
            at = slice(part * W, (part + 1) * W)
            add = jnp.dot(coef, cols[part], preferred_element_type=F32)
            acc[:, at] = add if first else acc[:, at] + add

    for s in range(1, 8):
        deliver(s).start()
    perm_t[...] = jnp.where(i1.astype(F32) == to_column(pos), F32(1.0), F32(0.0))
    for s in range(1, 4):
        deliver(s).wait_recv()
    for k in range(3):
        for b in range(3):
            over_link(b, k, 0).start()
    for s in range(4, 8):
        deliver(s).wait_recv()
    for k in range(3):
        for b in range(3):
            over_link(b, k, 1).start()
    to_sibling(0).start()
    absorb(0, 0, first=True)
    for k in range(3):
        for b in range(3):
            arrive(b, k, 0)
    to_sibling(0).wait_recv()
    absorb(1, 0)
    for k in range(3):
        for b in range(3):
            arrive(b, k, 1)
    for b in range(3):
        to_sibling(1 << b).start()
    todo = [(c, 1 << b) for c in range(2) for b in range(3)]
    for k in range(3, 6):
        for half in range(2):
            for b in range(3):
                arrive(b, k, half)
            c, h = todo.pop(0)
            if c == 1:
                to_sibling(h).wait_recv()
            absorb(c, h)
    pairs = (3, 5, 6)
    for h in pairs:
        to_sibling(h).start()
    for c in range(2):
        for h in pairs:
            if c == 1:
                to_sibling(h).wait_recv()
            absorb(c, h)
            if c == 1 and h == 3:
                for half in range(2):
                    for b in range(3):
                        arrive(b, 6, half)
                to_sibling(7).start()
    absorb(0, 7)
    to_sibling(7).wait_recv()
    absorb(1, 7)

    total = acc[...]
    top = jnp.max(jnp.abs(total), axis=1, keepdims=True)
    scale = (jnp.maximum(top, 1e-30) * (1.015625 / 32767.0)).astype(BF16).astype(F32)
    dens_col = jnp.sum(dacc[...], axis=1, keepdims=True)
    pay[0:1, :] = to_lanes(dens_col)
    pay[1:2, :] = to_lanes(scale)
    coded[...] = jnp.floor(total * (1.0 / scale) + 0.5).astype(jnp.int32).astype(jnp.int16)

    def give_back(s):
        return pltpu.make_async_remote_copy(
            src_ref=coded.at[pl.ds(s * SLICE, SLICE), :],
            dst_ref=back.at[pl.ds(s * SLICE, SLICE), :],
            send_sem=ret_send.at[s], recv_sem=ret_recv.at[s],
            device_id=outer[s], device_id_type=MESH)

    def give_pay(s):
        return pltpu.make_async_remote_copy(
            src_ref=pay, dst_ref=back_pay.at[s],
            send_sem=pay_send.at[s], recv_sem=pay_recv.at[s],
            device_id=outer[s], device_id_type=MESH)

    for s in range(7, 0, -1):
        give_back(s).start()
        give_pay(s).start()
    back[0:SLICE, :] = coded[0:SLICE, :]
    back_pay[0] = pay[...]
    for s in range(7, 0, -1):
        give_pay(s).wait_recv()

    block = lax.broadcasted_iota(jnp.int32, (8, ROWS), 1) // SLICE
    got = jnp.zeros((8, ROWS), F32)
    for s in range(8):
        got = jnp.where(block == s, back_pay[s], got)
    dens_row, scale_row = got[0:1, :], got[1:2, :]
    d1 = dens_row.astype(BF16)
    rest = dens_row - d1.astype(F32)
    d2 = rest.astype(BF16)
    d3 = (rest - d2.astype(F32)).astype(BF16)
    lift = lambda v: jnp.broadcast_to(v.astype(F32), (16, ROWS))
    which = lax.broadcasted_iota(jnp.int32, (16, ROWS), 0)
    terms = jnp.where(which == 0, lift(d1), jnp.where(which == 1, lift(d2), jnp.where(which == 2, lift(d3), F32(0.0))))
    spread = jnp.dot(terms.astype(BF16), perm[...], preferred_element_type=F32)
    dens_ref[...] = jnp.sum(spread, axis=0, keepdims=True)
    placed = (perm_t[...] * scale_row).astype(BF16)

    for s in range(7, 0, -1):
        give_back(s).wait_recv()
    for part in range(PARTS):
        at = slice(part * W, (part + 1) * W)
        value = back[:, at].astype(jnp.int32).astype(F32)
        high = value.astype(BF16)
        low = (value - high.astype(F32)).astype(BF16)
        out_ref[:, at] = jnp.dot(placed, high, preferred_element_type=F32) + jnp.dot(
            placed, low, preferred_element_type=F32)

    for s in range(1, 8):
        deliver(s).wait_send()
        give_back(s).wait_send()
        give_pay(s).wait_send()
    for b in range(3):
        for k in range(7):
            for half in range(2):
                over_link(b, k, half).wait_send()
    for h in range(8):
        to_sibling(h).wait_send()


def on_device(embeddings, cluster_ids):
    dma = pltpu.SemaphoreType.DMA
    total, dens = pl.pallas_call(
        kernel,
        out_shape=(jax.ShapeDtypeStruct((ROWS, D), F32), jax.ShapeDtypeStruct((1, ROWS), F32)),
        in_specs=[pl.BlockSpec(memory_space=pltpu.VMEM)] * 2,
        out_specs=(pl.BlockSpec(memory_space=pltpu.VMEM), pl.BlockSpec(memory_space=pltpu.VMEM)),
        scratch_shapes=[
            pltpu.VMEM((PARTS, ROWS, W), BF16),
            pltpu.VMEM((2, PARTS, 8, ROWS, W), BF16),
            pltpu.VMEM((ROWS, D), F32),
            pltpu.VMEM((ROWS, 128), F32),
            pltpu.VMEM((ROWS, ROWS), BF16),
            pltpu.VMEM((ROWS, ROWS), F32),
            pltpu.VMEM((ROWS, 128), F32),
            pltpu.VMEM((ROWS, D), jnp.int16),
            pltpu.VMEM((8, ROWS), F32),
            pltpu.VMEM((ROWS, D), jnp.int16),
            pltpu.VMEM((8, 8, ROWS), F32),
            dma((8,)), dma((8,)),
            dma((3, 7, 2)), dma((3, 7, 2)),
            dma((8,)), dma((8,)),
            dma((8,)), dma((8,)),
            dma((8,)), dma((8,)),
        ],
        compiler_params=pltpu.CompilerParams(
            collective_id=0, has_side_effects=True, vmem_limit_bytes=40 * 1024 * 1024),
        cost_estimate=pl.CostEstimate(
            flops=4 * ROWS * 4096 * D, bytes_accessed=3 * ROWS * D * 2, transcendentals=ROWS * 4096),
    )(embeddings, cluster_ids.reshape(1, ROWS))
    return total, dens.reshape(ROWS)


def solution(mesh):
    in_specs = (P(("gr", "gc"), None), P(("gr", "gc")))
    out_specs = (P(("gr", "gc"), None), P(("gr", "gc")))
    return jax.shard_map(
        on_device, mesh=mesh, in_specs=in_specs, out_specs=out_specs, check_vma=False
    )
```

```python
import functools

import jax
import jax.numpy as jnp
from jax import lax
from jax.experimental import pallas as pl
from jax.experimental.pallas import tpu as pltpu
from jax.sharding import PartitionSpec as P

MESH = pl.DeviceIdType.MESH
F32 = jnp.float32
BF16 = jnp.bfloat16

beta_scale = 16.0
ROWS = 256
D = 768
PARTS = 2
W = D // PARTS
SLICE = 32
HALF = ROWS // 2
SPLIT = 2
GROUPS = ((0, 32), (32, 96), (128, 128))
ORDER = (0, 1, 2, 4, 3, 5, 6, 7)


def place():
    gr, gc = lax.axis_index("gr"), lax.axis_index("gc")
    x = gc // 4
    y = ((gc // 2) % 2) * 2 + gr % 2
    z = gr // 2
    return x, y, z, gc % 2


def device(x, y, z, core):
    return (z * 2 + y % 2, x * 4 + (y // 2) * 2 + core)


def near(v):
    return v + 1 - 2 * (v % 2)


def far(v):
    return 3 - v


ITEMS = (((0, 0), (1, 0), (1, 2)), ((1, 0), (0, 0), (0, 1)))


def to_lanes(column):
    return jnp.transpose(jnp.broadcast_to(column, (column.shape[0], 128)))[0:1, :]


def to_column(row):
    return jnp.transpose(jnp.broadcast_to(row, (128, row.shape[1])))[:, 0:1]


def kernel(
    e_hbm, ids_hbm, out_ref, dens_ref,
    e_ref, ids_ref, load_sem, sorted_ref, held, across_rows, acc, dacc, perm, perm_t, inv_ref, coded, pay, back, back_pay,
    deliver_send, deliver_recv, link_send, link_recv, core_send, core_recv,
    ret_send, ret_recv, pay_send, pay_recv,
):
    x, y, z, core = place()
    here = (x, y, z)
    outer = []
    for s in range(8):
        t = [far(here[a]) if (ORDER[s] >> a) & 1 else here[a] for a in range(3)]
        outer.append(device(*t, core))
    inner = []
    for a in range(3):
        t = [near(here[i]) if i == a else here[i] for i in range(3)]
        inner.append(device(*t, core))
    sibling = device(x, y, z, 1 - core)
    across = []
    for s in range(8):
        t = [far(here[a]) if (ORDER[s] >> a) & 1 else here[a] for a in range(3)]
        t[SPLIT] = near(t[SPLIT])
        across.append(device(*t, core))
    holders = (outer, across)

    barrier = pltpu.get_barrier_semaphore()
    for d in outer[1:] + inner + [sibling] + across[1:]:
        pl.semaphore_signal(barrier, inc=1, device_id=d, device_id_type=MESH)

    loads = [pltpu.make_async_copy(ids_hbm, ids_ref, load_sem.at[0]),
             pltpu.make_async_copy(e_hbm, e_ref, load_sem.at[1])]
    for load in loads:
        load.start()

    mine = x // 2 + 2 * (y // 2) + 4 * (z // 2)
    loads[0].wait()
    rel = jnp.bitwise_xor(ids_ref[...], mine)
    slot = jnp.where(rel == 3, 4, jnp.where(rel == 4, 3, rel)).astype(F32)
    slot_col = to_column(slot)
    i0 = lax.broadcasted_iota(jnp.int32, (ROWS, ROWS), 0)
    i1 = lax.broadcasted_iota(jnp.int32, (ROWS, ROWS), 1)
    earlier = jnp.where((slot_col == slot) & (i0 < i1), F32(1.0), F32(0.0))
    pos = slot * SLICE + jnp.sum(earlier, axis=0, keepdims=True)
    p = jnp.where(i0.astype(F32) == pos, F32(1.0), F32(0.0)).astype(BF16)
    perm[...] = p
    loads[1].wait()
    rows = jnp.dot(p, e_ref[...], preferred_element_type=F32).astype(BF16)
    sorted_ref[...] = rows
    held[0, 0, 0:SLICE, :] = rows[0:SLICE]

    pl.semaphore_wait(barrier, 18)

    def deliver(s):
        return pltpu.make_async_remote_copy(
            src_ref=sorted_ref.at[pl.ds(s * SLICE, SLICE), :],
            dst_ref=held.at[0, 0, pl.ds(s * SLICE, SLICE), :],
            send_sem=deliver_send.at[s], recv_sem=deliver_recv.at[s],
            device_id=outer[s], device_id_type=MESH)

    def over_link(b, k, g):
        rows = pl.ds(*GROUPS[g])
        if b == SPLIT:
            source, target = held.at[0, 0, rows, :], across_rows.at[rows, :]
        else:
            part, h = ITEMS[b][k]
            cols = pl.ds(part * W, W)
            source, target = held.at[0, h, rows, cols], held.at[0, h ^ (1 << b), rows, cols]
        return pltpu.make_async_remote_copy(
            src_ref=source, dst_ref=target,
            send_sem=link_send.at[b, k, g], recv_sem=link_recv.at[b, k, g],
            device_id=inner[b], device_id_type=MESH)

    def to_sibling(h, half):
        rows = pl.ds(half * HALF, HALF)
        return pltpu.make_async_remote_copy(
            src_ref=held.at[0, h, rows, :], dst_ref=held.at[1, h, rows, :],
            send_sem=core_send.at[h, half], recv_sem=core_recv.at[h, half],
            device_id=sibling, device_id_type=MESH)

    def piece_to_sibling(part, h, g):
        rows, cols = pl.ds(*GROUPS[g]), pl.ds(part * W, W)
        return pltpu.make_async_remote_copy(
            src_ref=held.at[0, h, rows, cols], dst_ref=held.at[1, h, rows, cols],
            send_sem=core_send.at[h, g // 2], recv_sem=core_recv.at[h, g // 2],
            device_id=sibling, device_id_type=MESH)

    def arrive(b, k, g):
        over_link(b, k, g).wait_recv()
        part, h = ITEMS[b][k]
        h ^= 1 << b
        if (part, h) in ITEMS[1 - b]:
            over_link(1 - b, ITEMS[1 - b].index((part, h)), g).start()
        piece_to_sibling(part, h, g).start()

    def row_inv(rows):
        wide = rows.astype(F32)
        return lax.rsqrt(jnp.sum(wide * wide, axis=1, keepdims=True) + 1e-06)

    def absorb(pieces, sides, first=False, steps=None):
        cols = jnp.concatenate([held[c, h, half * HALF:(half + 1) * HALF, :] for c, h, half in pieces], axis=0)
        inv_lanes = to_lanes(row_inv(cols))
        for side, start, size in steps or [(side, 0, ROWS) for side in sides]:
            own = slice(start, start + size)
            rows = slice(side * ROWS + start, side * ROWS + start + size)
            mine = held[0, 0, own, :] if side == 0 else across_rows[own, :]
            if first:
                inv_ref[rows, :] = jnp.broadcast_to(row_inv(mine), (size, 128))
            raw = lax.dot_general(mine, cols, (((1,), (1,)), ((), ())), preferred_element_type=F32)
            sim = raw * inv_ref[rows, 0:1] * inv_lanes
            weight = jnp.exp(beta_scale * (sim - 1.0))
            dens = weight[:, :128] + weight[:, 128:]
            coef = (weight * inv_lanes).astype(BF16)
            dacc[rows, :] = dens if first else dacc[rows, :] + dens
            add = jnp.dot(coef, cols, preferred_element_type=F32)
            acc[rows, :] = add if first else acc[rows, :] + add
            if steps:
                finish(side, start // HALF)

    def give_back(side, s):
        return pltpu.make_async_remote_copy(
            src_ref=coded.at[side, pl.ds(s * SLICE, SLICE), :],
            dst_ref=back.at[side, pl.ds(s * SLICE, SLICE), :],
            send_sem=ret_send.at[side, s], recv_sem=ret_recv.at[side, s],
            device_id=holders[side][s], device_id_type=MESH)

    def give_pay(side, s):
        return pltpu.make_async_remote_copy(
            src_ref=pay.at[side, s // 4], dst_ref=back_pay.at[side, s],
            send_sem=pay_send.at[side, s], recv_sem=pay_recv.at[side, s],
            device_id=holders[side][s], device_id_type=MESH)

    def leaves(side, s):
        return side == 1 or s > 0

    def finish(side, half):
        own = slice(half * HALF, (half + 1) * HALF)
        rows = slice(side * ROWS + half * HALF, side * ROWS + (half + 1) * HALF)
        total = acc[rows, :]
        top = jnp.max(jnp.abs(total), axis=1, keepdims=True)
        scale = (jnp.maximum(top, 1e-30) * (1.015625 / 32767.0)).astype(BF16).astype(F32)
        coded[side, own, :] = jnp.floor(total * (1.0 / scale) + 0.5).astype(jnp.int32).astype(jnp.int16)
        dens_col = jnp.sum(dacc[rows, :], axis=1, keepdims=True)
        pay[side, half, 0:1, :] = to_lanes(dens_col)
        pay[side, half, 1:2, :] = to_lanes(scale)
        for s in range(4 * half + 3, 4 * half - 1, -1):
            if leaves(side, s):
                give_back(side, s).start()
                give_pay(side, s).start()

    for s in range(1, 4):
        deliver(s).start()
    perm_t[...] = jnp.where(i1.astype(F32) == to_column(pos), F32(1.0), F32(0.0))
    def own(g):
        for k in range(2):
            for b in range(2):
                over_link(b, k, g).start()
            if k == 0:
                over_link(SPLIT, 0, g).start()

    def arrivals(ks, g):
        for k in ks:
            for b in range(2):
                arrive(b, k, g)

    def whole(c, h):
        return (c, h, 0), (c, h, 1)

    own(0)
    for s in range(1, 4):
        deliver(s).wait_send()
    for s in range(4, 8):
        deliver(s).start()
    for s in range(1, 4):
        deliver(s).wait_recv()
    own(1)
    to_sibling(0, 0).start()
    arrivals(range(2), 0)
    arrivals(range(2), 1)
    for s in range(4, 8):
        deliver(s).wait_recv()
    own(2)
    to_sibling(0, 1).start()
    absorb(whole(0, 0), (0,), first=True)
    arrivals((2,), 0)
    to_sibling(0, 0).wait_recv()
    to_sibling(0, 1).wait_recv()
    absorb(whole(1, 0), (0,))
    arrivals((2,), 1)
    for g in range(3):
        over_link(SPLIT, 0, g).wait_recv()
    absorb(whole(0, 0), (1,), first=True)
    arrivals(range(2), 2)
    absorb(whole(1, 0), (1,))
    absorb(whole(0, 1), (0, 1))
    absorb(whole(0, 2), (0, 1))
    for h in (1, 2):
        for half in range(2):
            to_sibling(h, half).wait_recv()
    absorb(whole(1, 1), (0, 1))
    absorb(whole(1, 2), (0, 1))
    to_sibling(3, 0).wait_recv()
    absorb(((0, 3, 0), (1, 3, 0)), (0, 1))
    arrivals((2,), 2)
    to_sibling(3, 1).wait_recv()
    absorb(((0, 3, 1), (1, 3, 1)), (0, 1),
           steps=((1, HALF, HALF), (0, HALF, HALF), (1, 0, HALF), (0, 0, HALF)))

    back[0, 0:SLICE, :] = coded[0, 0:SLICE, :]
    back_pay[0, 0] = pay[0, 0]
    block = lax.broadcasted_iota(jnp.int32, (2, HALF), 1) // SLICE
    dens_rows = [None, None]
    for half in (1, 0):
        cols = slice(half * HALF, (half + 1) * HALF)
        placed = []
        for side in range(2):
            got = jnp.zeros((2, HALF), F32)
            for j in range(4):
                s = 4 * half + j
                if leaves(side, s):
                    give_pay(side, s).wait_recv()
                got = jnp.where(block == j, back_pay[side, s], got)
            dens_rows[half] = got[0:1, :] if side == 0 else dens_rows[half] + got[0:1, :]
            placed.append((perm_t[:, cols] * got[1:2, :]).astype(BF16))
        placed = jnp.concatenate(placed, axis=1)
        for side in range(2):
            for s in range(4 * half, 4 * half + 4):
                if leaves(side, s):
                    give_back(side, s).wait_recv()
        for part in range(3):
            at = slice(part * 256, (part + 1) * 256)
            value = jnp.concatenate([back[side, cols, at].astype(jnp.int32).astype(F32) for side in range(2)], axis=0)
            high = value.astype(BF16)
            low = (value - high.astype(F32)).astype(BF16)
            add = jnp.dot(placed, high, preferred_element_type=F32) + jnp.dot(
                placed, low, preferred_element_type=F32)
            out_ref[:, at] = add if half else out_ref[:, at] + add
    dens_row = jnp.concatenate(dens_rows, axis=1)
    d1 = dens_row.astype(BF16)
    rest = dens_row - d1.astype(F32)
    d2 = rest.astype(BF16)
    d3 = (rest - d2.astype(F32)).astype(BF16)
    lift = lambda v: jnp.broadcast_to(v.astype(F32), (16, ROWS))
    which = lax.broadcasted_iota(jnp.int32, (16, ROWS), 0)
    terms = jnp.where(which == 0, lift(d1), jnp.where(which == 1, lift(d2), jnp.where(which == 2, lift(d3), F32(0.0))))
    spread = jnp.dot(terms.astype(BF16), perm[...], preferred_element_type=F32)
    dens_ref[...] = jnp.sum(spread, axis=0, keepdims=True)

    for s in range(4, 8):
        deliver(s).wait_send()
    for side in range(2):
        for s in range(8):
            if leaves(side, s):
                give_back(side, s).wait_send()
                give_pay(side, s).wait_send()
    for g in range(3):
        over_link(SPLIT, 0, g).wait_send()
        for b in range(2):
            for k in range(3):
                over_link(b, k, g).wait_send()
    for h in range(4):
        for half in range(2):
            to_sibling(h, half).wait_send()


def on_device(embeddings, cluster_ids):
    dma = pltpu.SemaphoreType.DMA
    total, dens = pl.pallas_call(
        kernel,
        out_shape=(jax.ShapeDtypeStruct((ROWS, D), F32), jax.ShapeDtypeStruct((1, ROWS), F32)),
        in_specs=[pl.BlockSpec(memory_space=pltpu.HBM)] * 2,
        out_specs=(pl.BlockSpec(memory_space=pltpu.VMEM), pl.BlockSpec(memory_space=pltpu.VMEM)),
        scratch_shapes=[
            pltpu.VMEM((ROWS, D), BF16),
            pltpu.VMEM((1, ROWS), jnp.int32),
            dma((2,)),
            pltpu.VMEM((ROWS, D), BF16),
            pltpu.VMEM((2, 4, ROWS, D), BF16),
            pltpu.VMEM((ROWS, D), BF16),
            pltpu.VMEM((2 * ROWS, D), F32),
            pltpu.VMEM((2 * ROWS, 128), F32),
            pltpu.VMEM((ROWS, ROWS), BF16),
            pltpu.VMEM((ROWS, ROWS), F32),
            pltpu.VMEM((2 * ROWS, 128), F32),
            pltpu.VMEM((2, ROWS, D), jnp.int16),
            pltpu.VMEM((2, 2, 2, HALF), F32),
            pltpu.VMEM((2, ROWS, D), jnp.int16),
            pltpu.VMEM((2, 8, 2, HALF), F32),
            dma((8,)), dma((8,)),
            dma((3, 3, 3)), dma((3, 3, 3)),
            dma((4, 2)), dma((4, 2)),
            dma((2, 8)), dma((2, 8)),
            dma((2, 8)), dma((2, 8)),
        ],
        compiler_params=pltpu.CompilerParams(
            collective_id=0, has_side_effects=True, vmem_limit_bytes=40 * 1024 * 1024),
        cost_estimate=pl.CostEstimate(
            flops=4 * ROWS * 4096 * D, bytes_accessed=3 * ROWS * D * 2, transcendentals=ROWS * 4096),
    )(pltpu.with_memory_space_constraint(embeddings, pltpu.HBM), pltpu.with_memory_space_constraint(cluster_ids.reshape(1, ROWS), pltpu.HBM))
    return total, dens.reshape(ROWS)


def solution(mesh):
    in_specs = (P(("gr", "gc"), None), P(("gr", "gc")))
    out_specs = (P(("gr", "gc"), None), P(("gr", "gc")))
    return jax.shard_map(
        on_device, mesh=mesh, in_specs=in_specs, out_specs=out_specs, check_vma=False
    )
```

```python
import functools

import jax
import jax.numpy as jnp
from jax import lax
from jax.experimental import pallas as pl
from jax.experimental.pallas import tpu as pltpu
from jax.sharding import PartitionSpec as P

MESH = pl.DeviceIdType.MESH
F32 = jnp.float32
BF16 = jnp.bfloat16

beta_scale = 16.0
ROWS = 256
D = 768
PARTS = 2
W = D // PARTS
SLICE = 32
HALF = ROWS // 2
SPLIT = 2
GROUPS = ((0, 32), (32, 96), (128, 128))
ORDER = (0, 1, 2, 4, 3, 5, 6, 7)


def place():
    gr, gc = lax.axis_index("gr"), lax.axis_index("gc")
    x = gc // 4
    y = ((gc // 2) % 2) * 2 + gr % 2
    z = gr // 2
    return y, z, x, gc % 2


def device(y, z, x, core):
    return (z * 2 + y % 2, x * 4 + (y // 2) * 2 + core)


def near(v):
    return 3 - v


def far(v):
    return v + 1 - 2 * (v % 2)


def block_bit(v):
    return (v // 2 + v % 2) % 2


ITEMS = (((0, 0), (1, 0), (1, 2)), ((1, 0), (0, 0), (0, 1)))


def to_lanes(column):
    return jnp.transpose(jnp.broadcast_to(column, (column.shape[0], 128)))[0:1, :]


def to_column(row):
    return jnp.transpose(jnp.broadcast_to(row, (128, row.shape[1])))[:, 0:1]


def kernel(
    e_hbm, ids_hbm, out_ref, dens_ref,
    e_ref, ids_ref, load_sem, sorted_ref, held, across_rows, acc, dacc, perm, perm_t, inv_ref, coded, pay, back, back_pay,
    deliver_send, deliver_recv, link_send, link_recv, core_send, core_recv,
    ret_send, ret_recv, pay_send, pay_recv,
):
    *here, core = place()
    outer = []
    for s in range(8):
        t = [far(here[a]) if (ORDER[s] >> a) & 1 else here[a] for a in range(3)]
        outer.append(device(*t, core))
    inner = []
    for a in range(3):
        t = [near(here[i]) if i == a else here[i] for i in range(3)]
        inner.append(device(*t, core))
    sibling = device(*here, 1 - core)
    across = []
    for s in range(8):
        t = [far(here[a]) if (ORDER[s] >> a) & 1 else here[a] for a in range(3)]
        t[SPLIT] = near(t[SPLIT])
        across.append(device(*t, core))
    holders = (outer, across)

    barrier = pltpu.get_barrier_semaphore()
    for d in outer[1:] + inner + [sibling] + across[1:]:
        pl.semaphore_signal(barrier, inc=1, device_id=d, device_id_type=MESH)

    loads = [pltpu.make_async_copy(ids_hbm, ids_ref, load_sem.at[0]),
             pltpu.make_async_copy(e_hbm, e_ref, load_sem.at[1])]
    for load in loads:
        load.start()

    mine = block_bit(here[0]) + 2 * block_bit(here[1]) + 4 * block_bit(here[2])
    loads[0].wait()
    rel = jnp.bitwise_xor(ids_ref[...], mine)
    slot = jnp.where(rel == 3, 4, jnp.where(rel == 4, 3, rel)).astype(F32)
    slot_col = to_column(slot)
    i0 = lax.broadcasted_iota(jnp.int32, (ROWS, ROWS), 0)
    i1 = lax.broadcasted_iota(jnp.int32, (ROWS, ROWS), 1)
    earlier = jnp.where((slot_col == slot) & (i0 < i1), F32(1.0), F32(0.0))
    pos = slot * SLICE + jnp.sum(earlier, axis=0, keepdims=True)
    p = jnp.where(i0.astype(F32) == pos, F32(1.0), F32(0.0)).astype(BF16)
    perm[...] = p
    loads[1].wait()
    rows = jnp.dot(p, e_ref[...], preferred_element_type=F32).astype(BF16)
    for part in range(PARTS):
        sorted_ref[part] = rows[:, part * W:(part + 1) * W]
        held[0, 0, part, 0:SLICE, :] = rows[0:SLICE, part * W:(part + 1) * W]

    pl.semaphore_wait(barrier, 18)

    def deliver(s):
        return pltpu.make_async_remote_copy(
            src_ref=sorted_ref.at[:, pl.ds(s * SLICE, SLICE), :],
            dst_ref=held.at[0, 0, :, pl.ds(s * SLICE, SLICE), :],
            send_sem=deliver_send.at[s], recv_sem=deliver_recv.at[s],
            device_id=outer[s], device_id_type=MESH)

    def over_link(b, k, g):
        rows = pl.ds(*GROUPS[g])
        if b == SPLIT:
            source, target = held.at[0, 0, :, rows, :], across_rows.at[:, rows, :]
        else:
            part, h = ITEMS[b][k]
            source, target = held.at[0, h, part, rows, :], held.at[0, h ^ (1 << b), part, rows, :]
        return pltpu.make_async_remote_copy(
            src_ref=source, dst_ref=target,
            send_sem=link_send.at[b, k, g], recv_sem=link_recv.at[b, k, g],
            device_id=inner[b], device_id_type=MESH)

    def to_sibling(h, half):
        rows = pl.ds(half * HALF, HALF)
        return pltpu.make_async_remote_copy(
            src_ref=held.at[0, h, :, rows, :], dst_ref=held.at[1, h, :, rows, :],
            send_sem=core_send.at[h, half], recv_sem=core_recv.at[h, half],
            device_id=sibling, device_id_type=MESH)

    def piece_to_sibling(part, h, g):
        rows = pl.ds(*GROUPS[g])
        return pltpu.make_async_remote_copy(
            src_ref=held.at[0, h, part, rows, :], dst_ref=held.at[1, h, part, rows, :],
            send_sem=core_send.at[h, g // 2], recv_sem=core_recv.at[h, g // 2],
            device_id=sibling, device_id_type=MESH)

    def arrive(b, k, g):
        over_link(b, k, g).wait_recv()
        part, h = ITEMS[b][k]
        h ^= 1 << b
        if (part, h) in ITEMS[1 - b]:
            over_link(1 - b, ITEMS[1 - b].index((part, h)), g).start()
        piece_to_sibling(part, h, g).start()

    def row_inv(rows):
        wide = rows.astype(F32)
        return lax.rsqrt(jnp.sum(wide * wide, axis=1, keepdims=True) + 1e-06)

    def absorb(pieces, sides, first=False, steps=None):
        cols = jnp.concatenate([
            jnp.concatenate([held[c, h, part, half * HALF:(half + 1) * HALF, :] for part in range(PARTS)], axis=1)
            for c, h, half in pieces], axis=0)
        inv_lanes = to_lanes(row_inv(cols))
        for side, start, size in steps or [(side, 0, ROWS) for side in sides]:
            own = slice(start, start + size)
            rows = slice(side * ROWS + start, side * ROWS + start + size)
            mine = jnp.concatenate([
                held[0, 0, part, own, :] if side == 0 else across_rows[part, own, :] for part in range(PARTS)], axis=1)
            if first:
                inv_ref[rows, :] = jnp.broadcast_to(row_inv(mine), (size, 128))
            raw = lax.dot_general(mine, cols, (((1,), (1,)), ((), ())), preferred_element_type=F32)
            sim = raw * inv_ref[rows, 0:1] * inv_lanes
            weight = jnp.exp(beta_scale * (sim - 1.0))
            dens = weight[:, :128] + weight[:, 128:]
            coef = (weight * inv_lanes).astype(BF16)
            dacc[rows, :] = dens if first else dacc[rows, :] + dens
            add = jnp.dot(coef, cols, preferred_element_type=F32)
            acc[rows, :] = add if first else acc[rows, :] + add
            if steps:
                finish(side, start // HALF)

    def give_back(side, s):
        return pltpu.make_async_remote_copy(
            src_ref=coded.at[side, pl.ds(s * SLICE, SLICE), :],
            dst_ref=back.at[side, pl.ds(s * SLICE, SLICE), :],
            send_sem=ret_send.at[side, s], recv_sem=ret_recv.at[side, s],
            device_id=holders[side][s], device_id_type=MESH)

    def give_pay(side, s):
        return pltpu.make_async_remote_copy(
            src_ref=pay.at[side, s // 4], dst_ref=back_pay.at[side, s],
            send_sem=pay_send.at[side, s], recv_sem=pay_recv.at[side, s],
            device_id=holders[side][s], device_id_type=MESH)

    def leaves(side, s):
        return side == 1 or s > 0

    def finish(side, half):
        own = slice(half * HALF, (half + 1) * HALF)
        rows = slice(side * ROWS + half * HALF, side * ROWS + (half + 1) * HALF)
        total = acc[rows, :]
        top = jnp.max(jnp.abs(total), axis=1, keepdims=True)
        scale = (jnp.maximum(top, 1e-30) * (1.015625 / 32767.0)).astype(BF16).astype(F32)
        coded[side, own, :] = jnp.floor(total * (1.0 / scale) + 0.5).astype(jnp.int32).astype(jnp.int16)
        dens_col = jnp.sum(dacc[rows, :], axis=1, keepdims=True)
        pay[side, half, 0:1, :] = to_lanes(dens_col)
        pay[side, half, 1:2, :] = to_lanes(scale)
        for s in range(4 * half + 3, 4 * half - 1, -1):
            if leaves(side, s):
                give_back(side, s).start()
                give_pay(side, s).start()

    for s in range(1, 4):
        deliver(s).start()
    perm_t[...] = jnp.where(i1.astype(F32) == to_column(pos), F32(1.0), F32(0.0))
    def own(g):
        for k in range(2):
            for b in range(2):
                over_link(b, k, g).start()
            if k == 0:
                over_link(SPLIT, 0, g).start()

    def arrivals(ks, g):
        for k in ks:
            for b in range(2):
                arrive(b, k, g)

    def whole(c, h):
        return (c, h, 0), (c, h, 1)

    own(0)
    for s in range(1, 4):
        deliver(s).wait_send()
    for s in range(4, 8):
        deliver(s).start()
    for s in range(1, 4):
        deliver(s).wait_recv()
    own(1)
    to_sibling(0, 0).start()
    arrivals(range(2), 0)
    arrivals(range(2), 1)
    for s in range(4, 8):
        deliver(s).wait_recv()
    own(2)
    to_sibling(0, 1).start()
    absorb(whole(0, 0), (0,), first=True)
    arrivals((2,), 0)
    to_sibling(0, 0).wait_recv()
    to_sibling(0, 1).wait_recv()
    absorb(whole(1, 0), (0,))
    arrivals((2,), 1)
    for g in range(3):
        over_link(SPLIT, 0, g).wait_recv()
    absorb(whole(0, 0), (1,), first=True)
    arrivals(range(2), 2)
    absorb(whole(1, 0), (1,))
    absorb(whole(0, 1), (0, 1))
    absorb(whole(0, 2), (0, 1))
    for h in (1, 2):
        for half in range(2):
            to_sibling(h, half).wait_recv()
    absorb(whole(1, 1), (0, 1))
    absorb(whole(1, 2), (0, 1))
    to_sibling(3, 0).wait_recv()
    absorb(((0, 3, 0), (1, 3, 0)), (0, 1))
    arrivals((2,), 2)
    to_sibling(3, 1).wait_recv()
    absorb(((0, 3, 1), (1, 3, 1)), (0, 1),
           steps=((1, HALF, HALF), (0, HALF, HALF), (1, 0, HALF), (0, 0, HALF)))

    back[0, 0:SLICE, :] = coded[0, 0:SLICE, :]
    back_pay[0, 0] = pay[0, 0]
    block = lax.broadcasted_iota(jnp.int32, (2, HALF), 1) // SLICE
    dens_rows = [None, None]
    for half in (1, 0):
        cols = slice(half * HALF, (half + 1) * HALF)
        placed = []
        for side in range(2):
            got = jnp.zeros((2, HALF), F32)
            for j in range(4):
                s = 4 * half + j
                if leaves(side, s):
                    give_pay(side, s).wait_recv()
                got = jnp.where(block == j, back_pay[side, s], got)
            dens_rows[half] = got[0:1, :] if side == 0 else dens_rows[half] + got[0:1, :]
            placed.append((perm_t[:, cols] * got[1:2, :]).astype(BF16))
        placed = jnp.concatenate(placed, axis=1)
        for side in range(2):
            for s in range(4 * half, 4 * half + 4):
                if leaves(side, s):
                    give_back(side, s).wait_recv()
        for part in range(3):
            at = slice(part * 256, (part + 1) * 256)
            value = jnp.concatenate([back[side, cols, at].astype(jnp.int32).astype(F32) for side in range(2)], axis=0)
            high = value.astype(BF16)
            low = (value - high.astype(F32)).astype(BF16)
            add = jnp.dot(placed, high, preferred_element_type=F32) + jnp.dot(
                placed, low, preferred_element_type=F32)
            out_ref[:, at] = add if half else out_ref[:, at] + add
    dens_row = jnp.concatenate(dens_rows, axis=1)
    d1 = dens_row.astype(BF16)
    rest = dens_row - d1.astype(F32)
    d2 = rest.astype(BF16)
    d3 = (rest - d2.astype(F32)).astype(BF16)
    lift = lambda v: jnp.broadcast_to(v.astype(F32), (16, ROWS))
    which = lax.broadcasted_iota(jnp.int32, (16, ROWS), 0)
    terms = jnp.where(which == 0, lift(d1), jnp.where(which == 1, lift(d2), jnp.where(which == 2, lift(d3), F32(0.0))))
    spread = jnp.dot(terms.astype(BF16), perm[...], preferred_element_type=F32)
    dens_ref[...] = jnp.sum(spread, axis=0, keepdims=True)

    for s in range(4, 8):
        deliver(s).wait_send()
    for side in range(2):
        for s in range(8):
            if leaves(side, s):
                give_back(side, s).wait_send()
                give_pay(side, s).wait_send()
    for g in range(3):
        over_link(SPLIT, 0, g).wait_send()
        for b in range(2):
            for k in range(3):
                over_link(b, k, g).wait_send()
    for h in range(4):
        for half in range(2):
            to_sibling(h, half).wait_send()


def on_device(embeddings, cluster_ids):
    dma = pltpu.SemaphoreType.DMA
    total, dens = pl.pallas_call(
        kernel,
        out_shape=(jax.ShapeDtypeStruct((ROWS, D), F32), jax.ShapeDtypeStruct((1, ROWS), F32)),
        in_specs=[pl.BlockSpec(memory_space=pltpu.HBM)] * 2,
        out_specs=(pl.BlockSpec(memory_space=pltpu.VMEM), pl.BlockSpec(memory_space=pltpu.VMEM)),
        scratch_shapes=[
            pltpu.VMEM((ROWS, D), BF16),
            pltpu.VMEM((1, ROWS), jnp.int32),
            dma((2,)),
            pltpu.VMEM((PARTS, ROWS, W), BF16),
            pltpu.VMEM((2, 4, PARTS, ROWS, W), BF16),
            pltpu.VMEM((PARTS, ROWS, W), BF16),
            pltpu.VMEM((2 * ROWS, D), F32),
            pltpu.VMEM((2 * ROWS, 128), F32),
            pltpu.VMEM((ROWS, ROWS), BF16),
            pltpu.VMEM((ROWS, ROWS), F32),
            pltpu.VMEM((2 * ROWS, 128), F32),
            pltpu.VMEM((2, ROWS, D), jnp.int16),
            pltpu.VMEM((2, 2, 2, HALF), F32),
            pltpu.VMEM((2, ROWS, D), jnp.int16),
            pltpu.VMEM((2, 8, 2, HALF), F32),
            dma((8,)), dma((8,)),
            dma((3, 3, 3)), dma((3, 3, 3)),
            dma((4, 2)), dma((4, 2)),
            dma((2, 8)), dma((2, 8)),
            dma((2, 8)), dma((2, 8)),
        ],
        compiler_params=pltpu.CompilerParams(
            collective_id=0, has_side_effects=True, vmem_limit_bytes=40 * 1024 * 1024),
        cost_estimate=pl.CostEstimate(
            flops=4 * ROWS * 4096 * D, bytes_accessed=3 * ROWS * D * 2, transcendentals=ROWS * 4096),
    )(pltpu.with_memory_space_constraint(embeddings, pltpu.HBM), pltpu.with_memory_space_constraint(cluster_ids.reshape(1, ROWS), pltpu.HBM))
    return total, dens.reshape(ROWS)


def solution(mesh):
    in_specs = (P(("gr", "gc"), None), P(("gr", "gc")))
    out_specs = (P(("gr", "gc"), None), P(("gr", "gc")))
    return jax.shard_map(
        on_device, mesh=mesh, in_specs=in_specs, out_specs=out_specs, check_vma=False
    )
```

```python
import functools

import jax
import jax.numpy as jnp
from jax import lax
from jax.experimental import pallas as pl
from jax.experimental.pallas import tpu as pltpu
from jax.sharding import PartitionSpec as P

MESH = pl.DeviceIdType.MESH
F32 = jnp.float32
BF16 = jnp.bfloat16

beta_scale = 16.0
ROWS = 256
D = 768
PARTS = 2
W = D // PARTS
SLICE = 32
HALF = ROWS // 2
SPLIT = 2
GROUPS = ((0, 32), (32, 96), (128, 128))
ORDER = (0, 1, 2, 4, 3, 5, 6, 7)


def place():
    gr, gc = lax.axis_index("gr"), lax.axis_index("gc")
    x = gc // 4
    y = ((gc // 2) % 2) * 2 + gr % 2
    z = gr // 2
    return y, z, x, gc % 2


def device(y, z, x, core):
    return (z * 2 + y % 2, x * 4 + (y // 2) * 2 + core)


def near(v):
    return 3 - v


def far(v):
    return v + 1 - 2 * (v % 2)


def block_bit(v):
    return (v // 2 + v % 2) % 2


ITEMS = (((0, 0), (1, 0), (1, 2)), ((1, 0), (0, 0), (0, 1)))


def to_lanes(column):
    return jnp.transpose(jnp.broadcast_to(column, (column.shape[0], 128)))[0:1, :]


def to_column(row):
    return jnp.transpose(jnp.broadcast_to(row, (128, row.shape[1])))[:, 0:1]


def kernel(
    e_hbm, ids_hbm, out_ref, dens_ref,
    e_ref, ids_ref, load_sem, sorted_ref, held, across_rows, acc, dacc, perm, perm_t, inv_ref, coded, pay, back, back_pay,
    deliver_send, deliver_recv, link_send, link_recv, core_send, core_recv,
    ret_send, ret_recv, pay_send, pay_recv,
):
    *here, core = place()
    outer = []
    for s in range(8):
        t = [far(here[a]) if (ORDER[s] >> a) & 1 else here[a] for a in range(3)]
        outer.append(device(*t, core))
    inner = []
    for a in range(3):
        t = [near(here[i]) if i == a else here[i] for i in range(3)]
        inner.append(device(*t, core))
    sibling = device(*here, 1 - core)
    across = []
    for s in range(8):
        t = [far(here[a]) if (ORDER[s] >> a) & 1 else here[a] for a in range(3)]
        t[SPLIT] = near(t[SPLIT])
        across.append(device(*t, core))
    holders = (outer, across)

    barrier = pltpu.get_barrier_semaphore()
    for d in outer[1:] + inner + [sibling] + across[1:]:
        pl.semaphore_signal(barrier, inc=1, device_id=d, device_id_type=MESH)

    loads = [pltpu.make_async_copy(ids_hbm, ids_ref, load_sem.at[0]),
             pltpu.make_async_copy(e_hbm, e_ref, load_sem.at[1])]
    for load in loads:
        load.start()

    mine = block_bit(here[0]) + 2 * block_bit(here[1]) + 4 * block_bit(here[2])
    loads[0].wait()
    rel = jnp.bitwise_xor(ids_ref[...], mine)
    slot = jnp.where(rel == 3, 4, jnp.where(rel == 4, 3, rel)).astype(F32)
    slot_col = to_column(slot)
    i0 = lax.broadcasted_iota(jnp.int32, (ROWS, ROWS), 0)
    i1 = lax.broadcasted_iota(jnp.int32, (ROWS, ROWS), 1)
    earlier = jnp.where((slot_col == slot) & (i0 < i1), F32(1.0), F32(0.0))
    pos = slot * SLICE + jnp.sum(earlier, axis=0, keepdims=True)
    p = jnp.where(i0.astype(F32) == pos, F32(1.0), F32(0.0)).astype(BF16)
    perm[...] = p
    loads[1].wait()
    rows = jnp.dot(p, e_ref[...], preferred_element_type=F32).astype(BF16)
    for part in range(PARTS):
        sorted_ref[part] = rows[:, part * W:(part + 1) * W]
        held[0, 0, part, 0:SLICE, :] = rows[0:SLICE, part * W:(part + 1) * W]

    pl.semaphore_wait(barrier, 18)

    def deliver(s):
        return pltpu.make_async_remote_copy(
            src_ref=sorted_ref.at[:, pl.ds(s * SLICE, SLICE), :],
            dst_ref=held.at[0, 0, :, pl.ds(s * SLICE, SLICE), :],
            send_sem=deliver_send.at[s], recv_sem=deliver_recv.at[s],
            device_id=outer[s], device_id_type=MESH)

    def over_link(b, k, g):
        rows = pl.ds(*GROUPS[g])
        if b == SPLIT:
            source, target = held.at[0, 0, :, rows, :], across_rows.at[:, rows, :]
        else:
            part, h = ITEMS[b][k]
            source, target = held.at[0, h, part, rows, :], held.at[0, h ^ (1 << b), part, rows, :]
        return pltpu.make_async_remote_copy(
            src_ref=source, dst_ref=target,
            send_sem=link_send.at[b, k, g], recv_sem=link_recv.at[b, k, g],
            device_id=inner[b], device_id_type=MESH)

    def to_sibling(h, half):
        rows = pl.ds(half * HALF, HALF)
        return pltpu.make_async_remote_copy(
            src_ref=held.at[0, h, :, rows, :], dst_ref=held.at[1, h, :, rows, :],
            send_sem=core_send.at[h, half], recv_sem=core_recv.at[h, half],
            device_id=sibling, device_id_type=MESH)

    def piece_to_sibling(part, h, g):
        rows = pl.ds(*GROUPS[g])
        return pltpu.make_async_remote_copy(
            src_ref=held.at[0, h, part, rows, :], dst_ref=held.at[1, h, part, rows, :],
            send_sem=core_send.at[h, g // 2], recv_sem=core_recv.at[h, g // 2],
            device_id=sibling, device_id_type=MESH)

    def arrive(b, k, g):
        over_link(b, k, g).wait_recv()
        part, h = ITEMS[b][k]
        h ^= 1 << b
        if (part, h) in ITEMS[1 - b]:
            over_link(1 - b, ITEMS[1 - b].index((part, h)), g).start()
        piece_to_sibling(part, h, g).start()

    def row_inv(rows):
        wide = rows.astype(F32)
        return lax.rsqrt(jnp.sum(wide * wide, axis=1, keepdims=True) + 1e-06)

    def absorb(pieces, sides, first=False, steps=None):
        cols = jnp.concatenate([
            jnp.concatenate([held[c, h, part, half * HALF:(half + 1) * HALF, :] for part in range(PARTS)], axis=1)
            for c, h, half in pieces], axis=0)
        inv_lanes = to_lanes(row_inv(cols))
        for side, start, size in steps or [(side, 0, ROWS) for side in sides]:
            own = slice(start, start + size)
            rows = slice(side * ROWS + start, side * ROWS + start + size)
            mine = jnp.concatenate([
                held[0, 0, part, own, :] if side == 0 else across_rows[part, own, :] for part in range(PARTS)], axis=1)
            if first:
                inv_ref[rows, :] = jnp.broadcast_to(row_inv(mine), (size, 128))
            raw = lax.dot_general(mine, cols, (((1,), (1,)), ((), ())), preferred_element_type=F32)
            sim = raw * inv_ref[rows, 0:1] * inv_lanes
            weight = jnp.exp(beta_scale * (sim - 1.0))
            dens = weight[:, :128] + weight[:, 128:]
            coef = (weight * inv_lanes).astype(BF16)
            dacc[rows, :] = dens if first else dacc[rows, :] + dens
            add = jnp.dot(coef, cols, preferred_element_type=F32)
            acc[rows, :] = add if first else acc[rows, :] + add
            if steps:
                finish(side, start // HALF)

    def give_back(side, s):
        return pltpu.make_async_remote_copy(
            src_ref=coded.at[side, pl.ds(s * SLICE, SLICE), :],
            dst_ref=back.at[side, pl.ds(s * SLICE, SLICE), :],
            send_sem=ret_send.at[side, s], recv_sem=ret_recv.at[side, s],
            device_id=holders[side][s], device_id_type=MESH)

    def give_pay(side, s):
        return pltpu.make_async_remote_copy(
            src_ref=pay.at[side, s // 4], dst_ref=back_pay.at[side, s],
            send_sem=pay_send.at[side, s], recv_sem=pay_recv.at[side, s],
            device_id=holders[side][s], device_id_type=MESH)

    def leaves(side, s):
        return side == 1 or s > 0

    def finish(side, half):
        own = slice(half * HALF, (half + 1) * HALF)
        rows = slice(side * ROWS + half * HALF, side * ROWS + (half + 1) * HALF)
        total = acc[rows, :]
        top = jnp.max(jnp.abs(total), axis=1, keepdims=True)
        scale = (jnp.maximum(top, 1e-30) * (1.015625 / 32767.0)).astype(BF16).astype(F32)
        coded[side, own, :] = jnp.floor(total * (1.0 / scale) + 0.5).astype(jnp.int32).astype(jnp.int16)
        dens_col = jnp.sum(dacc[rows, :], axis=1, keepdims=True)
        pay[side, half, 0:1, :] = to_lanes(dens_col)
        pay[side, half, 1:2, :] = to_lanes(scale)
        for s in range(4 * half + 3, 4 * half - 1, -1):
            if leaves(side, s):
                give_back(side, s).start()
                give_pay(side, s).start()

    for s in range(1, 4):
        deliver(s).start()
    perm_t[...] = jnp.where(i1.astype(F32) == to_column(pos), F32(1.0), F32(0.0))
    def own(g):
        for k in range(2):
            for b in range(2):
                over_link(b, k, g).start()
            if k == 0:
                over_link(SPLIT, 0, g).start()

    def arrivals(ks, g):
        for k in ks:
            for b in range(2):
                arrive(b, k, g)

    def whole(c, h):
        return (c, h, 0), (c, h, 1)

    own(0)
    for s in range(1, 4):
        deliver(s).wait_send()
    for s in range(4, 8):
        deliver(s).start()
    for s in range(1, 4):
        deliver(s).wait_recv()
    own(1)
    to_sibling(0, 0).start()
    arrivals(range(2), 0)
    arrivals(range(2), 1)
    for s in range(4, 8):
        deliver(s).wait_recv()
    own(2)
    to_sibling(0, 1).start()
    absorb(whole(0, 0), (0,), first=True)
    arrivals((2,), 0)
    to_sibling(0, 0).wait_recv()
    to_sibling(0, 1).wait_recv()
    absorb(whole(1, 0), (0,))
    arrivals((2,), 1)
    for g in range(3):
        over_link(SPLIT, 0, g).wait_recv()
    absorb(whole(0, 0), (1,), first=True)
    arrivals(range(2), 2)
    absorb(whole(1, 0), (1,))
    absorb(whole(0, 1), (0, 1))
    absorb(whole(0, 2), (0, 1))
    for h in (1, 2):
        for half in range(2):
            to_sibling(h, half).wait_recv()
    absorb(whole(1, 1), (0, 1))
    absorb(whole(1, 2), (0, 1))
    to_sibling(3, 0).wait_recv()
    absorb(((0, 3, 0), (1, 3, 0)), (0, 1))
    arrivals((2,), 2)
    to_sibling(3, 1).wait_recv()
    absorb(((0, 3, 1), (1, 3, 1)), (0, 1),
           steps=((1, HALF, HALF), (0, HALF, HALF), (1, 0, HALF), (0, 0, HALF)))

    back[0, 0:SLICE, :] = coded[0, 0:SLICE, :]
    back_pay[0, 0] = pay[0, 0]
    block = lax.broadcasted_iota(jnp.int32, (2, HALF), 1) // SLICE
    dens_rows = [None, None]
    for half in (1, 0):
        cols = slice(half * HALF, (half + 1) * HALF)
        placed = []
        for side in range(2):
            got = jnp.zeros((2, HALF), F32)
            for j in range(4):
                s = 4 * half + j
                if leaves(side, s):
                    give_pay(side, s).wait_recv()
                got = jnp.where(block == j, back_pay[side, s], got)
            dens_rows[half] = got[0:1, :] if side == 0 else dens_rows[half] + got[0:1, :]
            placed.append((perm_t[:, cols] * got[1:2, :]).astype(BF16))
        placed = jnp.concatenate(placed, axis=1)
        for side in range(2):
            for s in range(4 * half, 4 * half + 4):
                if leaves(side, s):
                    give_back(side, s).wait_recv()
        for part in range(3):
            at = slice(part * 256, (part + 1) * 256)
            value = jnp.concatenate([back[side, cols, at].astype(jnp.int32).astype(F32) for side in range(2)], axis=0)
            high = value.astype(BF16)
            low = (value - high.astype(F32)).astype(BF16)
            add = jnp.dot(placed, high, preferred_element_type=F32) + jnp.dot(
                placed, low, preferred_element_type=F32)
            out_ref[:, at] = add if half else out_ref[:, at] + add
    dens_row = jnp.concatenate(dens_rows, axis=1)
    d1 = dens_row.astype(BF16)
    rest = dens_row - d1.astype(F32)
    d2 = rest.astype(BF16)
    d3 = (rest - d2.astype(F32)).astype(BF16)
    lift = lambda v: jnp.broadcast_to(v.astype(F32), (16, ROWS))
    which = lax.broadcasted_iota(jnp.int32, (16, ROWS), 0)
    terms = jnp.where(which == 0, lift(d1), jnp.where(which == 1, lift(d2), jnp.where(which == 2, lift(d3), F32(0.0))))
    spread = jnp.dot(terms.astype(BF16), perm[...], preferred_element_type=F32)
    dens_ref[...] = jnp.sum(spread, axis=0, keepdims=True)

    for s in range(4, 8):
        deliver(s).wait_send()
    for side in range(2):
        for s in range(8):
            if leaves(side, s):
                give_back(side, s).wait_send()
                give_pay(side, s).wait_send()
    for g in range(3):
        over_link(SPLIT, 0, g).wait_send()
        for b in range(2):
            for k in range(3):
                over_link(b, k, g).wait_send()
    for h in range(4):
        for half in range(2):
            to_sibling(h, half).wait_send()


def write_out(total, dens, total_out, dens_out, sems):
    copies = [pltpu.make_async_copy(total, total_out, sems.at[0]), pltpu.make_async_copy(dens, dens_out, sems.at[1])]
    for copy in copies:
        copy.start()
    for copy in copies:
        copy.wait()


def on_device(embeddings, cluster_ids):
    dma = pltpu.SemaphoreType.DMA
    total, dens = pl.pallas_call(
        kernel,
        out_shape=(jax.ShapeDtypeStruct((ROWS, D), F32), jax.ShapeDtypeStruct((1, ROWS), F32)),
        in_specs=[pl.BlockSpec(memory_space=pltpu.HBM)] * 2,
        out_specs=(pl.BlockSpec(memory_space=pltpu.VMEM), pl.BlockSpec(memory_space=pltpu.VMEM)),
        scratch_shapes=[
            pltpu.VMEM((ROWS, D), BF16),
            pltpu.VMEM((1, ROWS), jnp.int32),
            dma((2,)),
            pltpu.VMEM((PARTS, ROWS, W), BF16),
            pltpu.VMEM((2, 4, PARTS, ROWS, W), BF16),
            pltpu.VMEM((PARTS, ROWS, W), BF16),
            pltpu.VMEM((2 * ROWS, D), F32),
            pltpu.VMEM((2 * ROWS, 128), F32),
            pltpu.VMEM((ROWS, ROWS), BF16),
            pltpu.VMEM((ROWS, ROWS), F32),
            pltpu.VMEM((2 * ROWS, 128), F32),
            pltpu.VMEM((2, ROWS, D), jnp.int16),
            pltpu.VMEM((2, 2, 2, HALF), F32),
            pltpu.VMEM((2, ROWS, D), jnp.int16),
            pltpu.VMEM((2, 8, 2, HALF), F32),
            dma((8,)), dma((8,)),
            dma((3, 3, 3)), dma((3, 3, 3)),
            dma((4, 2)), dma((4, 2)),
            dma((2, 8)), dma((2, 8)),
            dma((2, 8)), dma((2, 8)),
        ],
        compiler_params=pltpu.CompilerParams(
            collective_id=0, has_side_effects=True, vmem_limit_bytes=40 * 1024 * 1024),
        cost_estimate=pl.CostEstimate(
            flops=4 * ROWS * 4096 * D, bytes_accessed=3 * ROWS * D * 2, transcendentals=ROWS * 4096),
    )(pltpu.with_memory_space_constraint(embeddings, pltpu.HBM), pltpu.with_memory_space_constraint(cluster_ids.reshape(1, ROWS), pltpu.HBM))
    total, dens = pl.pallas_call(
        write_out,
        out_shape=(jax.ShapeDtypeStruct((ROWS, D), F32), jax.ShapeDtypeStruct((1, ROWS), F32)),
        in_specs=[pl.BlockSpec(memory_space=pltpu.VMEM)] * 2,
        out_specs=(pl.BlockSpec(memory_space=pl.ANY), pl.BlockSpec(memory_space=pl.ANY)),
        scratch_shapes=[dma((2,))],
        compiler_params=pltpu.CompilerParams(vmem_limit_bytes=4 * 1024 * 1024),
    )(total, dens)
    return total, dens.reshape(ROWS)


def solution(mesh):
    in_specs = (P(("gr", "gc"), None), P(("gr", "gc")))
    out_specs = (P(("gr", "gc"), None), P(("gr", "gc")))
    return jax.shard_map(
        on_device, mesh=mesh, in_specs=in_specs, out_specs=out_specs, check_vma=False
    )
```

```python
import functools

import jax
import jax.numpy as jnp
from jax import lax
from jax.experimental import pallas as pl
from jax.experimental.pallas import tpu as pltpu
from jax.sharding import PartitionSpec as P

MESH = pl.DeviceIdType.MESH
F32 = jnp.float32
BF16 = jnp.bfloat16

beta_scale = 16.0
ROWS = 256
D = 768
PARTS = 2
W = D // PARTS
SLICE = 32
HALF = ROWS // 2
SPLIT = 2
GROUPS = ((0, 32), (32, 96), (128, 128))
ORDER = (0, 1, 2, 4, 3, 5, 6, 7)


def place():
    gr, gc = lax.axis_index("gr"), lax.axis_index("gc")
    x = gc // 4
    y = ((gc // 2) % 2) * 2 + gr % 2
    z = gr // 2
    return y, z, x, gc % 2


def device(y, z, x, core):
    return (z * 2 + y % 2, x * 4 + (y // 2) * 2 + core)


def near(v):
    return 3 - v


def far(v):
    return v + 1 - 2 * (v % 2)


def block_bit(v):
    return (v // 2 + v % 2) % 2


ITEMS = (((0, 0), (1, 0), (1, 2)), ((1, 0), (0, 0), (0, 1)))


def to_lanes(column):
    return jnp.transpose(jnp.broadcast_to(column, (column.shape[0], 128)))[0:1, :]


def to_column(row):
    return jnp.transpose(jnp.broadcast_to(row, (128, row.shape[1])))[:, 0:1]


def kernel(
    e_hbm, ids_hbm, out_ref, dens_ref,
    e_ref, ids_ref, load_sem, sorted_ref, held, across_rows, acc, dacc, perm, perm_t, inv_ref, coded, pay, back, back_pay,
    deliver_send, deliver_recv, link_send, link_recv, core_send, core_recv,
    ret_send, ret_recv, pay_send, pay_recv,
):
    *here, core = place()
    outer = []
    for s in range(8):
        t = [far(here[a]) if (ORDER[s] >> a) & 1 else here[a] for a in range(3)]
        outer.append(device(*t, core))
    inner = []
    for a in range(3):
        t = [near(here[i]) if i == a else here[i] for i in range(3)]
        inner.append(device(*t, core))
    sibling = device(*here, 1 - core)
    across = []
    for s in range(8):
        t = [far(here[a]) if (ORDER[s] >> a) & 1 else here[a] for a in range(3)]
        t[SPLIT] = near(t[SPLIT])
        across.append(device(*t, core))
    holders = (outer, across)

    barrier = pltpu.get_barrier_semaphore()
    for d in outer[1:] + inner + [sibling] + across[1:]:
        pl.semaphore_signal(barrier, inc=1, device_id=d, device_id_type=MESH)

    loads = [pltpu.make_async_copy(ids_hbm, ids_ref, load_sem.at[0]),
             pltpu.make_async_copy(e_hbm, e_ref, load_sem.at[1])]
    for load in loads:
        load.start()

    mine = block_bit(here[0]) + 2 * block_bit(here[1]) + 4 * block_bit(here[2])
    loads[0].wait()
    rel = jnp.bitwise_xor(ids_ref[...], mine)
    slot = jnp.where(rel == 3, 4, jnp.where(rel == 4, 3, rel)).astype(F32)
    slot_col = to_column(slot)
    i0 = lax.broadcasted_iota(jnp.int32, (ROWS, ROWS), 0)
    i1 = lax.broadcasted_iota(jnp.int32, (ROWS, ROWS), 1)
    earlier = jnp.where((slot_col == slot) & (i0 < i1), F32(1.0), F32(0.0))
    pos = slot * SLICE + jnp.sum(earlier, axis=0, keepdims=True)
    p = jnp.where(i0.astype(F32) == pos, F32(1.0), F32(0.0)).astype(BF16)
    perm[...] = p
    loads[1].wait()
    rows = jnp.dot(p, e_ref[...], preferred_element_type=F32).astype(BF16)
    for part in range(PARTS):
        sorted_ref[part] = rows[:, part * W:(part + 1) * W]
        held[0, 0, part, 0:SLICE, :] = rows[0:SLICE, part * W:(part + 1) * W]

    pl.semaphore_wait(barrier, 18)

    def deliver(s):
        return pltpu.make_async_remote_copy(
            src_ref=sorted_ref.at[:, pl.ds(s * SLICE, SLICE), :],
            dst_ref=held.at[0, 0, :, pl.ds(s * SLICE, SLICE), :],
            send_sem=deliver_send.at[s], recv_sem=deliver_recv.at[s],
            device_id=outer[s], device_id_type=MESH)

    def over_link(b, k, g):
        rows = pl.ds(*GROUPS[g])
        if b == SPLIT:
            rows = pl.ds((g - 1) * HALF, HALF)
            source, target = held.at[0, 0, :, rows, :], across_rows.at[:, rows, :]
        else:
            part, h = ITEMS[b][k]
            source, target = held.at[0, h, part, rows, :], held.at[0, h ^ (1 << b), part, rows, :]
        return pltpu.make_async_remote_copy(
            src_ref=source, dst_ref=target,
            send_sem=link_send.at[b, k, g], recv_sem=link_recv.at[b, k, g],
            device_id=inner[b], device_id_type=MESH)

    def to_sibling(h, half):
        rows = pl.ds(half * HALF, HALF)
        return pltpu.make_async_remote_copy(
            src_ref=held.at[0, h, :, rows, :], dst_ref=held.at[1, h, :, rows, :],
            send_sem=core_send.at[h, half], recv_sem=core_recv.at[h, half],
            device_id=sibling, device_id_type=MESH)

    def piece_to_sibling(part, h, g):
        rows = pl.ds(*GROUPS[g])
        return pltpu.make_async_remote_copy(
            src_ref=held.at[0, h, part, rows, :], dst_ref=held.at[1, h, part, rows, :],
            send_sem=core_send.at[h, g // 2], recv_sem=core_recv.at[h, g // 2],
            device_id=sibling, device_id_type=MESH)

    def arrive(b, k, g):
        over_link(b, k, g).wait_recv()
        part, h = ITEMS[b][k]
        h ^= 1 << b
        if (part, h) in ITEMS[1 - b]:
            over_link(1 - b, ITEMS[1 - b].index((part, h)), g).start()
        piece_to_sibling(part, h, g).start()

    def row_inv(rows):
        wide = rows.astype(F32)
        return lax.rsqrt(jnp.sum(wide * wide, axis=1, keepdims=True) + 1e-06)

    def absorb(pieces, sides, first=False, steps=None):
        cols = jnp.concatenate([
            jnp.concatenate([held[c, h, part, half * HALF:(half + 1) * HALF, :] for part in range(PARTS)], axis=1)
            for c, h, half in pieces], axis=0)
        inv_lanes = to_lanes(row_inv(cols))
        for side, start, size in steps or [(side, 0, ROWS) for side in sides]:
            own = slice(start, start + size)
            rows = slice(side * ROWS + start, side * ROWS + start + size)
            mine = jnp.concatenate([
                held[0, 0, part, own, :] if side == 0 else across_rows[part, own, :] for part in range(PARTS)], axis=1)
            if first:
                inv_ref[rows, :] = jnp.broadcast_to(row_inv(mine), (size, 128))
            raw = lax.dot_general(mine, cols, (((1,), (1,)), ((), ())), preferred_element_type=F32)
            sim = raw * inv_ref[rows, 0:1] * inv_lanes
            weight = jnp.exp(beta_scale * (sim - 1.0))
            dens = weight[:, :128] + weight[:, 128:]
            coef = (weight * inv_lanes).astype(BF16)
            dacc[rows, :] = dens if first else dacc[rows, :] + dens
            add = jnp.dot(coef, cols, preferred_element_type=F32)
            acc[rows, :] = add if first else acc[rows, :] + add
            if steps:
                finish(side, start // HALF)

    def give_back(side, s):
        return pltpu.make_async_remote_copy(
            src_ref=coded.at[side, pl.ds(s * SLICE, SLICE), :],
            dst_ref=back.at[side, pl.ds(s * SLICE, SLICE), :],
            send_sem=ret_send.at[side, s], recv_sem=ret_recv.at[side, s],
            device_id=holders[side][s], device_id_type=MESH)

    def give_pay(side, s):
        return pltpu.make_async_remote_copy(
            src_ref=pay.at[side, s // 4], dst_ref=back_pay.at[side, s],
            send_sem=pay_send.at[side, s], recv_sem=pay_recv.at[side, s],
            device_id=holders[side][s], device_id_type=MESH)

    def leaves(side, s):
        return side == 1 or s > 0

    def finish(side, half):
        own = slice(half * HALF, (half + 1) * HALF)
        rows = slice(side * ROWS + half * HALF, side * ROWS + (half + 1) * HALF)
        total = acc[rows, :]
        top = jnp.max(jnp.abs(total), axis=1, keepdims=True)
        scale = (jnp.maximum(top, 1e-30) * (1.015625 / 32767.0)).astype(BF16).astype(F32)
        coded[side, own, :] = jnp.floor(total * (1.0 / scale) + 0.5).astype(jnp.int32).astype(jnp.int16)
        dens_col = jnp.sum(dacc[rows, :], axis=1, keepdims=True)
        pay[side, half, 0:1, :] = to_lanes(dens_col)
        pay[side, half, 1:2, :] = to_lanes(scale)
        for s in range(4 * half + 3, 4 * half - 1, -1):
            if leaves(side, s):
                give_back(side, s).start()
                give_pay(side, s).start()

    for s in range(1, 4):
        deliver(s).start()
    perm_t[...] = jnp.where(i1.astype(F32) == to_column(pos), F32(1.0), F32(0.0))
    def own(g):
        for k in range(2):
            for b in range(2):
                over_link(b, k, g).start()
            if k == 0 and g > 0:
                over_link(SPLIT, 0, g).start()

    def arrivals(ks, g):
        for k in ks:
            for b in range(2):
                arrive(b, k, g)

    def whole(c, h):
        return (c, h, 0), (c, h, 1)

    own(0)
    for s in range(1, 4):
        deliver(s).wait_send()
    for s in range(4, 8):
        deliver(s).start()
    for s in range(1, 4):
        deliver(s).wait_recv()
    own(1)
    to_sibling(0, 0).start()
    arrivals(range(2), 0)
    arrivals(range(2), 1)
    for s in range(4, 8):
        deliver(s).wait_recv()
    own(2)
    to_sibling(0, 1).start()
    absorb(whole(0, 0), (0,), first=True)
    arrivals((2,), 0)
    to_sibling(0, 0).wait_recv()
    to_sibling(0, 1).wait_recv()
    absorb(whole(1, 0), (0,))
    arrivals((2,), 1)
    for g in range(1, 3):
        over_link(SPLIT, 0, g).wait_recv()
    absorb(whole(0, 0), (1,), first=True)
    arrivals(range(2), 2)
    absorb(whole(1, 0), (1,))
    absorb(whole(0, 1), (0, 1))
    absorb(whole(0, 2), (0, 1))
    for h in (1, 2):
        for half in range(2):
            to_sibling(h, half).wait_recv()
    absorb(whole(1, 1), (0, 1))
    absorb(whole(1, 2), (0, 1))
    to_sibling(3, 0).wait_recv()
    absorb(((0, 3, 0), (1, 3, 0)), (0, 1))
    arrivals((2,), 2)
    to_sibling(3, 1).wait_recv()
    absorb(((0, 3, 1), (1, 3, 1)), (0, 1),
           steps=((1, HALF, HALF), (0, HALF, HALF), (1, 0, HALF), (0, 0, HALF)))

    back[0, 0:SLICE, :] = coded[0, 0:SLICE, :]
    back_pay[0, 0] = pay[0, 0]
    block = lax.broadcasted_iota(jnp.int32, (2, HALF), 1) // SLICE
    dens_rows = [None, None]
    for half in (1, 0):
        cols = slice(half * HALF, (half + 1) * HALF)
        placed = []
        for side in range(2):
            got = jnp.zeros((2, HALF), F32)
            for j in range(4):
                s = 4 * half + j
                if leaves(side, s):
                    give_pay(side, s).wait_recv()
                got = jnp.where(block == j, back_pay[side, s], got)
            dens_rows[half] = got[0:1, :] if side == 0 else dens_rows[half] + got[0:1, :]
            placed.append((perm_t[:, cols] * got[1:2, :]).astype(BF16))
        placed = jnp.concatenate(placed, axis=1)
        for side in range(2):
            for s in range(4 * half, 4 * half + 4):
                if leaves(side, s):
                    give_back(side, s).wait_recv()
        for part in range(3):
            at = slice(part * 256, (part + 1) * 256)
            value = jnp.concatenate([back[side, cols, at].astype(jnp.int32).astype(F32) for side in range(2)], axis=0)
            high = value.astype(BF16)
            low = (value - high.astype(F32)).astype(BF16)
            add = jnp.dot(placed, high, preferred_element_type=F32) + jnp.dot(
                placed, low, preferred_element_type=F32)
            out_ref[:, at] = add if half else out_ref[:, at] + add
    dens_row = jnp.concatenate(dens_rows, axis=1)
    d1 = dens_row.astype(BF16)
    rest = dens_row - d1.astype(F32)
    d2 = rest.astype(BF16)
    d3 = (rest - d2.astype(F32)).astype(BF16)
    lift = lambda v: jnp.broadcast_to(v.astype(F32), (16, ROWS))
    which = lax.broadcasted_iota(jnp.int32, (16, ROWS), 0)
    terms = jnp.where(which == 0, lift(d1), jnp.where(which == 1, lift(d2), jnp.where(which == 2, lift(d3), F32(0.0))))
    spread = jnp.dot(terms.astype(BF16), perm[...], preferred_element_type=F32)
    dens_ref[...] = jnp.sum(spread, axis=0, keepdims=True)

    for s in range(4, 8):
        deliver(s).wait_send()
    for side in range(2):
        for s in range(8):
            if leaves(side, s):
                give_back(side, s).wait_send()
                give_pay(side, s).wait_send()
    for g in range(3):
        if g > 0:
            over_link(SPLIT, 0, g).wait_send()
        for b in range(2):
            for k in range(3):
                over_link(b, k, g).wait_send()
    for h in range(4):
        for half in range(2):
            to_sibling(h, half).wait_send()


def write_out(total, dens, total_out, dens_out, sems):
    copies = [pltpu.make_async_copy(total, total_out, sems.at[0]), pltpu.make_async_copy(dens, dens_out, sems.at[1])]
    for copy in copies:
        copy.start()
    for copy in copies:
        copy.wait()


def on_device(embeddings, cluster_ids):
    dma = pltpu.SemaphoreType.DMA
    total, dens = pl.pallas_call(
        kernel,
        out_shape=(jax.ShapeDtypeStruct((ROWS, D), F32), jax.ShapeDtypeStruct((1, ROWS), F32)),
        in_specs=[pl.BlockSpec(memory_space=pltpu.HBM)] * 2,
        out_specs=(pl.BlockSpec(memory_space=pltpu.VMEM), pl.BlockSpec(memory_space=pltpu.VMEM)),
        scratch_shapes=[
            pltpu.VMEM((ROWS, D), BF16),
            pltpu.VMEM((1, ROWS), jnp.int32),
            dma((2,)),
            pltpu.VMEM((PARTS, ROWS, W), BF16),
            pltpu.VMEM((2, 4, PARTS, ROWS, W), BF16),
            pltpu.VMEM((PARTS, ROWS, W), BF16),
            pltpu.VMEM((2 * ROWS, D), F32),
            pltpu.VMEM((2 * ROWS, 128), F32),
            pltpu.VMEM((ROWS, ROWS), BF16),
            pltpu.VMEM((ROWS, ROWS), F32),
            pltpu.VMEM((2 * ROWS, 128), F32),
            pltpu.VMEM((2, ROWS, D), jnp.int16),
            pltpu.VMEM((2, 2, 2, HALF), F32),
            pltpu.VMEM((2, ROWS, D), jnp.int16),
            pltpu.VMEM((2, 8, 2, HALF), F32),
            dma((8,)), dma((8,)),
            dma((3, 3, 3)), dma((3, 3, 3)),
            dma((4, 2)), dma((4, 2)),
            dma((2, 8)), dma((2, 8)),
            dma((2, 8)), dma((2, 8)),
        ],
        compiler_params=pltpu.CompilerParams(
            collective_id=0, has_side_effects=True, vmem_limit_bytes=40 * 1024 * 1024),
        cost_estimate=pl.CostEstimate(
            flops=4 * ROWS * 4096 * D, bytes_accessed=3 * ROWS * D * 2, transcendentals=ROWS * 4096),
    )(pltpu.with_memory_space_constraint(embeddings, pltpu.HBM), pltpu.with_memory_space_constraint(cluster_ids.reshape(1, ROWS), pltpu.HBM))
    total, dens = pl.pallas_call(
        write_out,
        out_shape=(jax.ShapeDtypeStruct((ROWS, D), F32), jax.ShapeDtypeStruct((1, ROWS), F32)),
        in_specs=[pl.BlockSpec(memory_space=pltpu.VMEM)] * 2,
        out_specs=(pl.BlockSpec(memory_space=pl.ANY), pl.BlockSpec(memory_space=pl.ANY)),
        scratch_shapes=[dma((2,))],
        compiler_params=pltpu.CompilerParams(vmem_limit_bytes=4 * 1024 * 1024),
    )(total, dens)
    return total, dens.reshape(ROWS)


def solution(mesh):
    in_specs = (P(("gr", "gc"), None), P(("gr", "gc")))
    out_specs = (P(("gr", "gc"), None), P(("gr", "gc")))
    return jax.shard_map(
        on_device, mesh=mesh, in_specs=in_specs, out_specs=out_specs, check_vma=False
    )
```
